256 devices in a mesh: frame: 64 (over x, y, z_lo), mp: 4 (over z_hi, core).
Axes of the slice: x: 4, y: 4, z: 8 (z_hi: 2, z_lo: 4; z = z_hi * 4 + z_lo), core: 2. Of those that a mesh axis runs over, the one named last changes fastest.
Arguments:
- kf_query: bfloat16 [4096, 4096], P('frame', 'mp'), may hold values from -6 to 6
- kf_kv: bfloat16 [2, 4096, 4096], P(None, 'frame', 'mp'), may hold values from -6 to 6
- cache_kv: bfloat16 [2, 16384, 4096], P(None, 'frame', 'mp'), may hold values from -6 to 6
- kf_latent: bfloat16 [4096, 4096], P('frame', 'mp'), may hold values from -6 to 6
- lift_weight: bfloat16 [4096, 8192], P('mp', 'frame'), may hold values from -0.09375 to 0.09375
- gap_latent: bfloat16 [256, 16, 16, 8192], P('frame', None, None, 'mp'), may hold values from -6 to 6
- query_map: bfloat16 [64, 128, 128], P('mp'), may hold values from -1 to 1
- key_map: bfloat16 [64, 128, 128], P('mp'), may hold values from -10 to 10
- frame_counts: int32 [256], P('frame'), may hold values from 1 to 16, as said below
- noise_step: int32 [1], replicated, may hold values from 200 to 800
Outputs:
- kf_out: bfloat16 [4096, 4096], P('frame', 'mp')
- gap_out: bfloat16 [256, 16, 16, 8192], P('frame', None, None, 'mp')
The draws below stay inside these ranges and needn't reach their ends.
Inputs may be any that keep to these rules, and one draw needn't show every extreme that they name: `frame_counts`: some gap has 16 frames and some gap has 1.
All inputs are finite; a program needn't handle non-finite values.
Results may differ from the reference program's by a relative error of at most 0.0044.
Values may be sent and summed in bfloat16 or wider, within the bound.
No kernel may reach another device: no remote copies, remote signals or barrier semaphores. Data moves between devices by JAX's collectives and lax.ppermute only.
A program may use at most 128 MiB of HBM per device.

```python
import math
import jax
import jax.numpy as jnp
from jax import lax

D = 4096
E = 8192
HD = 128
GAPF = 16
STRIDE = 200
KF_DEV = 4
TOKF = 16
CTX = 256
KEYFRAMES = 256
KEYTOK = 4096
NCTX = 16384
N_FRAME = 64


def draw_frame_counts(key, part):
    key = jax.random.fold_in(key, 11)
    counts = jax.random.randint(key, (KEYFRAMES,), 1, GAPF + 1)
    return counts.at[0].set(GAPF).at[KEYFRAMES - 1].set(1).astype(jnp.int32)


def draw_kf_query(key, part):
    key = jax.random.fold_in(key, 23)
    values = jnp.clip(jax.random.normal(key, (KEYTOK, D), jnp.float32), -6.0, 6.0)
    return values.astype(jnp.bfloat16)


def draw_kf_kv(key, part):
    key = jax.random.fold_in(key, 29)
    values = jnp.clip(jax.random.normal(key, (2, KEYTOK, D), jnp.float32), -6.0, 6.0)
    return values.astype(jnp.bfloat16)


def draw_gap_latent(key, part):
    key = jax.random.fold_in(key, 41)
    values = jnp.clip(jax.random.normal(key, (KEYFRAMES, GAPF, TOKF, E), jnp.float32), -6.0, 6.0)
    return values.astype(jnp.bfloat16)


def map_pair(key):
    heads = E // HD
    base = jnp.clip(jax.random.normal(jax.random.fold_in(key, 301), (heads, HD, HD), jnp.float32), -2.5, 2.5) * HD ** (-0.5)
    return base


def draw_query_map(key, part):
    base = map_pair(key)
    return base.astype(jnp.bfloat16)


def draw_key_map(key, part):
    key = jax.random.fold_in(key, 37)
    heads = E // HD
    values = jnp.clip(jax.random.normal(key, (heads, HD, HD), jnp.float32), -2.5, 2.5) * HD ** (-0.5)
    return values.astype(jnp.bfloat16)


def level_of(stream_key, extent, cuts, least, largest):
    def one(position, parts):
        steps = jax.random.uniform(jax.random.fold_in(jax.random.fold_in(stream_key, 6), position), (parts,), jnp.float32, least / len(cuts), largest / len(cuts))
        return jnp.repeat(jnp.exp(steps), extent[position] // parts).reshape((-1,) + (1,) * (len(extent) - position - 1))

    gain = one(*cuts[0])
    for cut in cuts[1:]:
        gain = gain * one(*cut)
    return gain


def centred(rng, extent, spread, bound, cuts=(), held_as=jnp.bfloat16):
    level = level_of(rng, extent, cuts, -0.22, 0.18) if cuts else 1.0
    drawn = jax.random.normal(rng, extent, jnp.float32) * spread * level
    return jnp.minimum(jnp.maximum(drawn, -bound), bound).astype(held_as)


def setup_inputs(seed: int = 0) -> dict:
    key_list = jax.random.split(jax.random.key(seed), 11)
    return {
        "kf_query": draw_kf_query(jax.random.fold_in(key_list[10], 71), 0),
        "kf_kv": draw_kf_kv(jax.random.fold_in(key_list[10], 71), 0),
        "cache_kv": centred(key_list[2], (2, NCTX, D), 1.0, 6.0, ((1, 64), (2, 4))),
        "kf_latent": centred(key_list[3], (KEYTOK, D), 1.0, 6.0, ((0, 64), (1, 4))),
        "lift_weight": centred(key_list[4], (D, E), D ** -0.5, 0.09375, ((0, 4), (1, 64))),
        "gap_latent": draw_gap_latent(jax.random.fold_in(key_list[10], 71), 0),
        "query_map": draw_query_map(jax.random.fold_in(key_list[10], 71), 0),
        "key_map": draw_key_map(jax.random.fold_in(key_list[10], 71), 0),
        "frame_counts": draw_frame_counts(jax.random.fold_in(key_list[10], 71), 0),
        "noise_step": jax.random.randint(key_list[9], (1,), STRIDE, 801).astype(jnp.int32),
    }


def attend(queries, key_rows, value_rows, usable, heads):
    count_q = queries.shape[0]
    count_k = key_rows.shape[0]
    query_h = queries.reshape(count_q, heads, HD).astype(jnp.float32)
    key_h = key_rows.reshape(count_k, heads, HD).astype(jnp.float32)
    value_h = value_rows.reshape(count_k, heads, HD).astype(jnp.float32)
    scores = jnp.einsum('qhd,khd->hqk', query_h, key_h) * HD ** (-0.5)
    scores = jnp.where(usable[None], scores, -1e+30)
    highest = lax.optimization_barrier(jnp.max(scores, axis=2, keepdims=True))
    probs = jnp.exp(scores - highest)
    totals = lax.optimization_barrier(jnp.sum(probs, axis=2))
    weights = lax.optimization_barrier(probs.astype(jnp.bfloat16)).astype(jnp.float32)
    mixed = jnp.einsum('hqk,khd->qhd', weights, value_h)
    return (mixed / jnp.transpose(totals)[:, :, None]).reshape(count_q, heads * HD)

def head_map(rows, maps):
    count = rows.shape[0]
    heads = maps.shape[0]
    split = rows.reshape(count, heads, HD).astype(jnp.float32)
    mapped = jnp.einsum('nhd,hde->nhe', split, maps.astype(jnp.float32))
    return mapped.reshape(count, heads * HD).astype(jnp.bfloat16)

def signal_level(step):
    return jnp.cos((step / 1000.0 + 0.008) / 1.008 * (math.pi / 2)) ** 2

def denoise(latent, left, right, count, query_map, key_map, level_now, level_prev):
    frames = latent.shape[0]
    tokf = latent.shape[1]
    width = latent.shape[2]
    heads = query_map.shape[0]
    index = jnp.arange(frames, dtype=jnp.int32)
    along = ((index + 1).astype(jnp.float32) / (count + 1).astype(jnp.float32))[:, None, None]
    noisy = latent.astype(jnp.float32)
    inputs = (noisy + (1.0 - along) * left.astype(jnp.float32)[None] + along * right.astype(jnp.float32)[None]).astype(jnp.bfloat16)
    tokens = inputs.reshape(frames * tokf, width)
    value_rows = jnp.concatenate([tokens, left, right], 0)
    queries = head_map(tokens, query_map)
    key_rows = head_map(value_rows, key_map)
    live = index < count
    usable = jnp.concatenate([jnp.repeat(live, tokf), jnp.ones((2 * tokf,), bool)])[None]
    guess = attend(queries, key_rows, value_rows, usable, heads).reshape(frames, tokf, width)
    clean = (noisy - jnp.sqrt(1.0 - level_now) * guess) / jnp.sqrt(level_now)
    stepped = jnp.sqrt(level_prev) * clean + jnp.sqrt(1.0 - level_prev) * guess
    return jnp.where(live[:, None, None], stepped, 0.0).astype(jnp.bfloat16)

def reference(kf_query, kf_kv, cache_kv, kf_latent, lift_weight, gap_latent, query_map, key_map, frame_counts, noise_step):
    block_rows = KF_DEV * TOKF
    padded = jnp.pad(cache_kv, ((0, 0), (CTX, CTX), (0, 0)))

    def key_block(block):
        queries = lax.dynamic_slice_in_dim(kf_query, block * block_rows, block_rows, 0)
        context = lax.dynamic_slice_in_dim(padded, block * CTX, 3 * CTX, 1)
        own = lax.dynamic_slice_in_dim(kf_kv, block * block_rows, block_rows, 1)
        places = block * CTX - CTX + jnp.arange(3 * CTX, dtype=jnp.int32)
        inside = (places >= 0) & (places < NCTX)
        usable = jnp.concatenate([inside, jnp.ones((block_rows,), bool)])[None]
        key_rows = jnp.concatenate([context[0], own[0]], 0)
        value_rows = jnp.concatenate([context[1], own[1]], 0)
        result = attend(queries, key_rows, value_rows, usable, D // HD)
        latent = lax.dynamic_slice_in_dim(kf_latent, block * block_rows, block_rows, 0)
        return (latent.astype(jnp.float32) + result).astype(jnp.bfloat16)
    kf_out = lax.map(key_block, jnp.arange(N_FRAME, dtype=jnp.int32)).reshape(KEYTOK, D)
    lifted = jnp.dot(kf_out, lift_weight, preferred_element_type=jnp.float32).astype(jnp.bfloat16)
    lifted_k = lifted.reshape(KEYFRAMES, TOKF, E)
    right_all = jnp.concatenate([lifted_k[1:], jnp.zeros((1, TOKF, E), jnp.bfloat16)], 0)
    step = noise_step[0].astype(jnp.float32)
    level_now = signal_level(step)
    level_prev = signal_level(step - STRIDE)

    def one_gap(items):
        latent, left, right, count = items
        return denoise(latent, left, right, count, query_map, key_map, level_now, level_prev)
    gap_out = lax.map(one_gap, (gap_latent, lifted_k, right_all, frame_counts))
    return (kf_out, gap_out)
```

```python
import functools
import math

import jax
import jax.numpy as jnp
from jax import lax
from jax.experimental import pallas as pl
from jax.experimental.pallas import tpu as pltpu
from jax.sharding import Mesh
from jax.sharding import PartitionSpec as P

HD = 128
STRIDE = 200
NEG = -1e30
BF = jnp.bfloat16
F32 = jnp.float32
SCALE = HD ** (-0.5)
SIZES = (4, 4, 4, 2, 2)
AXES = ("x", "y", "z", "h", "c")
FRAME = ("x", "y", "z")
N_FRAME = 64


def nt(a, b):
    return lax.dot_general(a, b, (((1,), (1,)), ((), ())), preferred_element_type=F32)


def nn(a, b):
    return jnp.dot(a, b, preferred_element_type=F32)


def kf_kernel(edge, q, kv, own, prev, nxt, latent, out):
    has_prev = edge[0] > 0
    has_next = edge[1] > 0
    for h in range(q.shape[1] // HD):
        cols = slice(h * HD, (h + 1) * HD)
        query = q[:, cols]
        scores = [
            jnp.where(has_prev, nt(query, prev[0, :, cols]) * SCALE, NEG),
            nt(query, own[0, :, cols]) * SCALE,
            jnp.where(has_next, nt(query, nxt[0, :, cols]) * SCALE, NEG),
            nt(query, kv[0, :, cols]) * SCALE,
        ]
        top = functools.reduce(jnp.maximum, [jnp.max(s, axis=1, keepdims=True) for s in scores])
        probs = [jnp.exp(s - top) for s in scores]
        total = sum(jnp.sum(p, axis=1, keepdims=True) for p in probs)
        mixed = sum(
            nn(p.astype(BF), v[1, :, cols]) for p, v in zip(probs, (prev, own, nxt, kv))
        )
        out[:, cols] = (latent[:, cols].astype(F32) + mixed / total).astype(BF)


def kf_attention(edge, q, kv, own, prev, nxt, latent):
    rows, width = q.shape
    ctx = own.shape[1]
    step = 2 * HD
    flat = pl.BlockSpec((rows, step), lambda i, e: (0, i))
    pair = pl.BlockSpec((2, rows, step), lambda i, e: (0, 0, i))
    wide = pl.BlockSpec((2, ctx, step), lambda i, e: (0, 0, i))
    return pl.pallas_call(
        kf_kernel,
        grid_spec=pltpu.PrefetchScalarGridSpec(
            num_scalar_prefetch=1,
            grid=(width // step,),
            in_specs=[flat, pair, wide, wide, wide, flat],
            out_specs=flat,
        ),
        out_shape=jax.ShapeDtypeStruct((rows, width), BF),
        cost_estimate=pl.CostEstimate(
            flops=4 * rows * width * (3 * ctx + rows),
            bytes_accessed=2 * (12 * ctx * width + 8 * rows * width) // 2,
            transcendentals=rows * (width // HD) * (3 * ctx + rows),
        ),
        name="kf_attention",
    )(edge, q, kv, own, prev, nxt, latent)


def lift_kernel(info, *refs):
    acts = refs[0:8]
    weights = refs[8:12]
    out = refs[12]
    rows, total = refs[13:]
    z = info[0]

    @pl.when(pl.program_id(0) == 0)
    def _():
        for s in range(2):
            for d in range(4):
                rows[s, d * 64 : (d + 1) * 64, :] = acts[s * 4 + d][...]

    total[...] = jnp.zeros_like(total)
    for d in range(4):
        total[info[5 + d]] += nn(rows[info[1 + d]], weights[d][0])
    for d in range(4):
        to = lax.rem(z + 4 - d, 4)
        for h in range(2):
            out[to * 2 + h] = total[h, d * 64 : (d + 1) * 64, :].astype(BF)


def lift(info, acts, weights):
    rows, width = acts[0].shape
    whole = pl.BlockSpec((rows, width), lambda i, e: (0, 0))
    tile = pl.BlockSpec((1, width, HD), lambda i, e: (i, 0, 0))
    return pl.pallas_call(
        lift_kernel,
        grid_spec=pltpu.PrefetchScalarGridSpec(
            num_scalar_prefetch=1,
            grid=(4,),
            in_specs=[whole] * 8 + [tile] * 4,
            out_specs=pl.BlockSpec((8, rows, HD), lambda i, e: (0, 0, i)),
            scratch_shapes=[
                pltpu.VMEM((2, 4 * rows, width), BF),
                pltpu.VMEM((2, 4 * rows, HD), F32),
            ],
        ),
        out_shape=jax.ShapeDtypeStruct((8, rows, 4 * HD), BF),
        cost_estimate=pl.CostEstimate(
            flops=2 * 4 * rows * 2 * width * 8 * HD,
            bytes_accessed=2 * (16 * width * HD + 8 * rows * width + 32 * rows * HD),
            transcendentals=0,
        ),
        name="lift",
    )(info, *acts, *weights)


def combine_kernel(parts, out, first):
    for z in range(4):
        for y in range(4):
            cols = slice(y * HD, (y + 1) * HD)
            place = slice((y * 4 + z) * HD, (y * 4 + z + 1) * HD)
            total = parts[2 * z, :, cols].astype(F32) + parts[2 * z + 1, :, cols].astype(F32)
            total = total.astype(BF)
            out[:, place] = total
            first[:, place] = total[: first.shape[0]]


def combine(parts, tokf):
    rows = parts.shape[1]
    width = 4 * parts.shape[2]
    return pl.pallas_call(
        combine_kernel,
        out_shape=(
            jax.ShapeDtypeStruct((rows, width), BF),
            jax.ShapeDtypeStruct((tokf, width), BF),
        ),
        cost_estimate=pl.CostEstimate(
            flops=2 * rows * width, bytes_accessed=6 * rows * width, transcendentals=0
        ),
        name="combine",
    )(parts)


def gap_kernel(first, heads, count, along, keep, move, latent, left, right, qmap, kmap, *rest):
    out = rest[-1]
    gap = first + pl.program_id(0)
    frames, tokf = latent.shape[1], latent.shape[2]
    toks = frames * tokf
    live = count[gap] * tokf
    keys = lax.broadcasted_iota(jnp.int32, (1, toks), 1)
    bias = jnp.where(keys < live, 0.0, NEG).astype(F32)
    ones_a = jnp.ones((toks, HD), BF)
    ones_b = jnp.ones((2 * tokf, HD), BF)
    for h in range(heads):
        cols = slice(h * HD, (h + 1) * HD)
        lo, hi = left[:, cols], right[:, cols]
        lo32, hi32 = lo.astype(F32), hi.astype(F32)
        tokens = jnp.concatenate(
            [
                (
                    latent[0, j, :, cols].astype(F32)
                    + (1.0 - along[gap, j]) * lo32
                    + along[gap, j] * hi32
                ).astype(BF)
                for j in range(frames)
            ],
            axis=0,
        )
        sides = jnp.concatenate([lo, hi], axis=0)
        mapped = nn(tokens, jnp.concatenate([qmap[h], kmap[h]], axis=1)).astype(BF)
        query, key = mapped[:, :HD], mapped[:, HD:]
        side_key = nn(sides, kmap[h]).astype(BF)
        sa = nt(query, key) + bias
        sb = nt(query, side_key)
        top = jnp.maximum(
            jnp.max(sa, axis=1, keepdims=True), jnp.max(sb, axis=1, keepdims=True)
        )
        pa = jnp.exp((sa - top) * SCALE).astype(BF)
        pb = jnp.exp((sb - top) * SCALE).astype(BF)
        mixed = nn(pa, jnp.concatenate([tokens, ones_a], axis=1)) + nn(
            pb, jnp.concatenate([sides, ones_b], axis=1)
        )
        guess = mixed[:, :HD] / mixed[:, HD:]
        for j in range(frames):
            rows = slice(j * tokf, (j + 1) * tokf)
            out[0, j, :, cols] = (
                latent[0, j, :, cols].astype(F32) * keep[gap, j] + guess[rows] * move[gap, j]
            ).astype(BF)


def denoise(first, gaps, tables, latent, left, right, qmap, kmap, heads=4, into=None):
    _, frames, tokf, width = latent.shape
    step = heads * HD
    spot = pl.BlockSpec((1, frames, tokf, step), lambda g, i, *s: (first + g, 0, 0, i))
    side = pl.BlockSpec((tokf, step), lambda g, i, *s: (g, i))
    maps = pl.BlockSpec((heads, HD, HD), lambda g, i, *s: (i, 0, 0))
    extra = [] if into is None else [into]
    specs = [spot, side, side, maps, maps] + [pl.BlockSpec(memory_space=pl.ANY)] * len(extra)
    toks = frames * tokf
    return pl.pallas_call(
        functools.partial(gap_kernel, first, heads),
        grid_spec=pltpu.PrefetchScalarGridSpec(
            num_scalar_prefetch=4,
            grid=(gaps, width // step),
            in_specs=specs,
            out_specs=spot,
        ),
        out_shape=jax.ShapeDtypeStruct(latent.shape, BF),
        input_output_aliases={9: 0} if extra else {},
        cost_estimate=pl.CostEstimate(
            flops=gaps * 2 * toks * width * (2 * HD + 2 * (toks + 2 * tokf)),
            bytes_accessed=4 * gaps * toks * width,
            transcendentals=gaps * (width // HD) * toks * (toks + 2 * tokf),
        ),
        name=f"denoise_{first}",
    )(*tables, latent, left, right, qmap, kmap, *extra)


def signal_level(step):
    return jnp.cos((step / 1000.0 + 0.008) / 1.008 * (math.pi / 2)) ** 2


def ring(size, by):
    return [(i, (i + by) % size) for i in range(size)]


def gather_weight(weight):
    pieces = [weight] + [lax.ppermute(weight, "y", ring(4, d)) for d in (1, 2, 3)]
    y = lax.axis_index("y")
    table = jnp.stack(pieces)
    table = jnp.take(table, (y - jnp.arange(4)) % 4, axis=0)
    moved = []
    for d in range(4):
        perm = [(a * 2 + b, ((a + d + b) % 4) * 2 + (a & 1)) for a in range(4) for b in range(2)]
        moved.append(lax.ppermute(table, ("x", "c"), perm))
    return moved


def on_device(
    kf_query,
    kf_kv,
    cache_kv,
    kf_latent,
    lift_weight,
    gap_latent,
    query_map,
    key_map,
    frame_counts,
    noise_step,
):
    x, y, z, h, c = (lax.axis_index(a) for a in AXES)
    frame = (x * 4 + y) * 4 + z
    up = [(i, i + 1) for i in range(N_FRAME - 1)]
    down = [(j, i) for i, j in up]
    prev = lax.ppermute(cache_kv, FRAME, up)
    nxt = lax.ppermute(cache_kv, FRAME, down)
    weights = gather_weight(lift_weight)

    edge = jnp.stack([frame > 0, frame < N_FRAME - 1]).astype(jnp.int32)
    updated = kf_attention(edge, kf_query, kf_kv, cache_kv, prev, nxt, kf_latent)

    mine = [updated] + [lax.ppermute(updated, "z", ring(4, d)) for d in (1, 2, 3)]
    theirs = [lax.ppermute(a, "c", ring(2, 1)) for a in mine]

    core = [(x - d - c) % 2 for d in range(4)]
    at = [(x - d - s) % 4 for d, s in zip(range(4), core)]
    info = jnp.stack(
        [z] + [(s != c).astype(jnp.int32) for s in core] + [a // 2 for a in at]
    ).astype(jnp.int32)
    parts = lift(info, mine + theirs, weights)
    parts = lax.all_to_all(parts, ("z", "h"), 0, 0, tiled=False)

    gaps, frames, tokf, width = gap_latent.shape
    lifted, initial = combine(parts, tokf)
    following = lax.ppermute(initial, FRAME, down)

    step = noise_step[0].astype(F32)
    now = signal_level(step)
    before = signal_level(step - STRIDE)
    slots = jnp.arange(frames, dtype=jnp.int32)[None]
    counts = frame_counts[:, None]
    along = (slots + 1).astype(F32) / (counts + 1).astype(F32)
    live = slots < counts
    keep = jnp.where(live, jnp.sqrt(before) / jnp.sqrt(now), 0.0)
    move = jnp.where(
        live, jnp.sqrt(1.0 - before) - jnp.sqrt(before) * jnp.sqrt(1.0 - now) / jnp.sqrt(now), 0.0
    )
    tables = (frame_counts, along, keep, move)
    inner = (gaps - 1) * tokf
    out = denoise(
        0, gaps - 1, tables, gap_latent, lifted[:inner], lifted[tokf:], query_map, key_map
    )
    out = denoise(
        gaps - 1, 1, tables, gap_latent, lifted[inner:], following, query_map, key_map, into=out
    )
    return updated, out


def solution(mesh):
    fine = Mesh(mesh.devices.reshape(SIZES), AXES)
    mp = ("h", "c")
    placed = (
        P(FRAME, mp),
        P(None, FRAME, mp),
        P(None, FRAME, mp),
        P(FRAME, mp),
        P(mp, FRAME),
        P(FRAME, None, None, mp),
        P(mp, None, None),
        P(mp, None, None),
        P(FRAME),
        P(),
    )
    return jax.shard_map(
        on_device,
        mesh=fine,
        in_specs=placed,
        out_specs=(P(FRAME, mp), P(FRAME, None, None, mp)),
        check_vma=False,
    )
```

```python
import functools
import math

import jax
import jax.numpy as jnp
from jax import lax
from jax.experimental import pallas as pl
from jax.experimental.pallas import tpu as pltpu
from jax.sharding import Mesh
from jax.sharding import PartitionSpec as P

HD = 128
STRIDE = 200
NEG = -1e30
BF = jnp.bfloat16
F32 = jnp.float32
SCALE = HD ** (-0.5)
SIZES = (4, 4, 4, 2, 2)
AXES = ("x", "y", "z", "h", "c")
FRAME = ("x", "y", "z")
N_FRAME = 64


def nt(a, b):
    return lax.dot_general(a, b, (((1,), (1,)), ((), ())), preferred_element_type=F32)


def tn(a, b):
    return lax.dot_general(a, b, (((0,), (0,)), ((), ())), preferred_element_type=F32)


def nn(a, b):
    return jnp.dot(a, b, preferred_element_type=F32)


def part_of(query, pairs, cols):
    scores = [nt(query, kv[0, :, cols]) for kv in pairs]
    top = functools.reduce(jnp.maximum, [jnp.max(s, axis=1, keepdims=True) for s in scores])
    probs = [jnp.exp((s - top) * SCALE) for s in scores]
    total = sum(jnp.sum(p, axis=1, keepdims=True) for p in probs)
    mixed = sum(nn(p.astype(BF), kv[1, :, cols]) for p, kv in zip(probs, pairs))
    return mixed * (1.0 / total), top * SCALE + jnp.log(total)


def own_kernel(q, kv, own, latent, out, logs, kept):
    step = pl.program_id(0)
    lane = lax.broadcasted_iota(jnp.int32, logs.shape, 1)

    @pl.when(step == 0)
    def _():
        logs[...] = jnp.zeros(logs.shape, F32)

    count = q.shape[1] // HD
    for h in range(count):
        cols = slice(h * HD, (h + 1) * HD)
        mixed, log = part_of(q[:, cols], (own, kv), cols)
        out[:, cols] = mixed
        logs[...] = jnp.where(lane == step * count + h, log, logs[...])
    kept[...] = latent[...]


def own_part(q, kv, own, latent):
    rows, width = q.shape
    ctx = own.shape[1]
    keys = kv.shape[1] + ctx
    step = 2 * HD
    flat = pl.BlockSpec((rows, step), lambda i: (0, i))
    return pl.pallas_call(
        own_kernel,
        grid=(width // step,),
        in_specs=[
            flat,
            pl.BlockSpec((2, rows, step), lambda i: (0, 0, i)),
            pl.BlockSpec((2, ctx, step), lambda i: (0, 0, i)),
            flat,
        ],
        out_specs=(flat, pl.BlockSpec((rows, HD), lambda i: (0, 0)), flat),
        out_shape=(
            jax.ShapeDtypeStruct((rows, width), F32),
            jax.ShapeDtypeStruct((rows, HD), F32),
            jax.ShapeDtypeStruct((rows, width), BF),
        ),
        cost_estimate=pl.CostEstimate(
            flops=4 * rows * width * keys,
            bytes_accessed=4 * keys * width + 6 * rows * width,
            transcendentals=rows * (width // HD) * keys,
        ),
        compiler_params=pltpu.CompilerParams(vmem_limit_bytes=56 << 20),
        name="own_part",
    )(q, kv, own, latent)


def far_kernel(q_a, q_b, own, out_a, out_b):
    rows, width = q_a.shape
    heads = width // HD
    lane = lax.broadcasted_iota(jnp.int32, (2 * rows, HD), 1)
    logs = jnp.zeros((2 * rows, HD), F32)
    for h in range(heads):
        cols = slice(h * HD, (h + 1) * HD)
        query = jnp.concatenate([q_a[:, cols], q_b[:, cols]], axis=0)
        mixed, log = part_of(query, (own,), cols)
        out_a[:, cols] = mixed[:rows].astype(BF)
        out_b[:, cols] = mixed[rows:].astype(BF)
        for k in range(3):
            piece = log.astype(BF).astype(F32)
            logs = jnp.where(lane == k * heads + h, piece, logs)
            log = log - piece
    out_a[:, width:] = logs[:rows].astype(BF)
    out_b[:, width:] = logs[rows:].astype(BF)


def far_parts(q_a, q_b, own):
    rows, width = q_a.shape
    keys = own.shape[1]
    shape = jax.ShapeDtypeStruct((rows, width + HD), BF)
    return pl.pallas_call(
        far_kernel,
        out_shape=(shape, shape),
        cost_estimate=pl.CostEstimate(
            flops=8 * rows * width * keys,
            bytes_accessed=4 * keys * width + 8 * rows * width,
            transcendentals=2 * rows * (width // HD) * keys,
        ),
        compiler_params=pltpu.CompilerParams(vmem_limit_bytes=16 << 20),
        name="far_parts",
    )(q_a, q_b, own)


def join_kernel(edge, latent, own, stat, before, after, out, moving):
    rows, width = latent.shape
    heads = width // HD

    def log_of(part, there):
        logs = part[:, width:].astype(F32)
        logs = logs + pltpu.roll(logs, HD - heads, 1) + pltpu.roll(logs, HD - 2 * heads, 1)
        return jnp.where(there, logs, NEG)

    logs = (stat[...], log_of(before, edge[0] > 0), log_of(after, edge[1] > 0))
    top = functools.reduce(jnp.maximum, logs)
    share = [jnp.exp(v - top) for v in logs]
    inverse = 1.0 / (share[0] + share[1] + share[2])
    share = [v * inverse for v in share]
    for h in range(heads):
        cols = slice(h * HD, (h + 1) * HD)
        one = slice(h, h + 1)
        attn = (
            own[:, cols] * share[0][:, one]
            + before[:, cols].astype(F32) * share[1][:, one]
            + after[:, cols].astype(F32) * share[2][:, one]
        )
        total = (latent[:, cols].astype(F32) + attn).astype(BF)
        out[:, cols] = total
        moving[:, cols] = total


def join(edge, latent, own, stat, before, after):
    rows, width = latent.shape
    vmem = pl.BlockSpec(memory_space=pltpu.VMEM)
    return pl.pallas_call(
        join_kernel,
        in_specs=[pl.BlockSpec(memory_space=pltpu.SMEM)] + [vmem] * 5,
        out_shape=(jax.ShapeDtypeStruct((rows, width), BF),) * 2,
        cost_estimate=pl.CostEstimate(
            flops=8 * rows * width, bytes_accessed=12 * rows * width, transcendentals=4 * rows * HD
        ),
        compiler_params=pltpu.CompilerParams(vmem_limit_bytes=56 << 20),
        name="join",
    )(edge, latent, own, stat, before, after)


def lift_kernel(info, *refs):
    acts, pieces = refs[0:4], refs[4:8]
    keep, send, rows = refs[8:]
    x, y, z, c = info[0], info[1], info[2], info[3]
    frame_rows = acts[0].shape[0]
    for d in range(4):
        rows[d * frame_rows : (d + 1) * frame_rows, :] = acts[d][...]
    for e in range(4):
        for pair in range(2):
            total = nn(
                rows[...],
                jnp.concatenate([pieces[e][2 * pair], pieces[e][2 * pair + 1]], axis=1),
            )
            for k in range(2):
                d = 2 * pair + k
                head_x = lax.rem(x + 4 - jnp.where(c == 0, e, d), 4)
                head_y = lax.rem(y + 4 - jnp.where(c == 0, d, e), 4)
                mine = lax.rem(head_x, 2) == c
                cols = pl.ds(pl.multiple_of(head_y * HD, HD), HD)

                def put(out, cast):
                    for f in range(4):
                        to = lax.rem(z + 4 - f, 4) * 2 + head_x // 2
                        part = total[f * frame_rows : (f + 1) * frame_rows]
                        out[to, :, cols] = cast(part[:, k * HD : (k + 1) * HD])

                @pl.when(mine)
                def _():
                    put(keep, lambda v: v)

                @pl.when(jnp.logical_not(mine))
                def _():
                    put(send, lambda v: v.astype(BF))


def lift(info, acts, pieces):
    rows, width = acts[0].shape
    vmem = pl.BlockSpec(memory_space=pltpu.VMEM)
    return pl.pallas_call(
        lift_kernel,
        in_specs=[pl.BlockSpec(memory_space=pltpu.SMEM)] + [vmem] * 8,
        out_shape=(
            jax.ShapeDtypeStruct((8, rows, 4 * HD), F32),
            jax.ShapeDtypeStruct((8, rows, 4 * HD), BF),
        ),
        scratch_shapes=[pltpu.VMEM((4 * rows, width), BF)],
        compiler_params=pltpu.CompilerParams(vmem_limit_bytes=24 << 20),
        cost_estimate=pl.CostEstimate(
            flops=2 * 4 * rows * width * 16 * HD,
            bytes_accessed=2 * (16 * width * HD + 4 * rows * width + 48 * rows * HD),
            transcendentals=0,
        ),
        name="lift",
    )(info, *acts, *pieces)


def combine_kernel(parts, out, first):
    for y in range(4):
        cols = slice(y * HD, (y + 1) * HD)
        for z in range(4):
            place = slice((y * 4 + z) * HD, (y * 4 + z + 1) * HD)
            total = parts[2 * z, :, cols].astype(F32) + parts[2 * z + 1, :, cols].astype(F32)
            total = total.astype(BF)
            out[:, place] = total
            first[:, place] = total[: first.shape[0]]


def combine(parts, tokf):
    rows = parts.shape[1]
    width = 4 * parts.shape[2]
    return pl.pallas_call(
        combine_kernel,
        out_shape=(
            jax.ShapeDtypeStruct((rows, width), BF),
            jax.ShapeDtypeStruct((tokf, width), BF),
        ),
        cost_estimate=pl.CostEstimate(
            flops=2 * rows * width, bytes_accessed=6 * rows * width, transcendentals=0
        ),
        compiler_params=pltpu.CompilerParams(vmem_limit_bytes=16 << 20),
        name="combine",
    )(parts)


def gap_kernel(first, count, along, keep, move, latent, left, right, qmap, kmap, *rest):
    out = rest[-1]
    gap = first + pl.program_id(0)
    heads = qmap.shape[0]
    frames, tokf = latent.shape[1], latent.shape[2]
    toks = frames * tokf
    live = count[gap] * tokf
    bias = jnp.where(lax.broadcasted_iota(jnp.int32, (toks, 1), 0) < live, 0.0, NEG).astype(F32)

    def map_rows(h):
        cols = slice(h * HD, (h + 1) * HD)
        lo, hi = left[:, cols], right[:, cols]
        lo32, hi32 = lo.astype(F32), hi.astype(F32)
        tokens = [
            (
                latent[0, j, :, cols].astype(F32)
                + (1.0 - along[gap, j]) * lo32
                + along[gap, j] * hi32
            ).astype(BF)
            for j in range(frames)
        ]
        values = jnp.concatenate(tokens + [lo, hi], axis=0)
        mapped = nn(values, jnp.concatenate([qmap[h], kmap[h]], axis=1)).astype(BF)
        return values, mapped[:toks, :HD], mapped[:, HD:]

    def score(values, query, key):
        scores = nt(key, query)
        return values, jnp.concatenate([scores[:toks] + bias, scores[toks:]], axis=0)

    def finish(h, values, scores):
        cols = slice(h * HD, (h + 1) * HD)
        top = jnp.max(scores, axis=0, keepdims=True)
        probs = jnp.exp2((scores - top) * (SCALE * math.log2(math.e)))
        total = jnp.sum(probs, axis=0, keepdims=True)
        mixed = tn(values, probs.astype(BF))
        guess = jnp.transpose(mixed * (1.0 / total))
        for j in range(frames):
            rows = slice(j * tokf, (j + 1) * tokf)
            out[0, j, :, cols] = (
                latent[0, j, :, cols].astype(F32) * keep[gap, j] + guess[rows] * move[gap, j]
            ).astype(BF)

    mapped, scored = {}, {}
    for t in range(heads + 2):
        if t < heads:
            mapped[t] = map_rows(t)
        if 0 <= t - 1 < heads:
            scored[t - 1] = score(*mapped.pop(t - 1))
        if 0 <= t - 2 < heads:
            finish(t - 2, *scored.pop(t - 2))


def denoise(first, gaps, tables, latent, left, right, right_at, qmap, kmap, into=None):
    _, frames, tokf, width = latent.shape
    heads = width // HD
    spot = pl.BlockSpec((1, frames, tokf, width), lambda g, *s: (first + g, 0, 0, 0))
    before = pl.BlockSpec((tokf, width), lambda g, *s: (first + g, 0))
    after = pl.BlockSpec((tokf, width), lambda g, *s: (right_at + g, 0))
    maps = pl.BlockSpec((heads, HD, HD), lambda g, *s: (0, 0, 0))
    extra = [] if into is None else [into]
    specs = [spot, before, after, maps, maps] + [pl.BlockSpec(memory_space=pl.ANY)] * len(extra)
    toks = frames * tokf
    return pl.pallas_call(
        functools.partial(gap_kernel, first),
        grid_spec=pltpu.PrefetchScalarGridSpec(
            num_scalar_prefetch=4, grid=(gaps,), in_specs=specs, out_specs=spot
        ),
        out_shape=jax.ShapeDtypeStruct(latent.shape, BF),
        input_output_aliases={9: 0} if extra else {},
        compiler_params=pltpu.CompilerParams(vmem_limit_bytes=52 << 20),
        cost_estimate=pl.CostEstimate(
            flops=gaps * 2 * toks * width * (2 * HD + 2 * (toks + 2 * tokf)),
            bytes_accessed=4 * gaps * toks * width,
            transcendentals=gaps * heads * toks * (toks + 2 * tokf),
        ),
        name=f"denoise_{first}",
    )(*tables, latent, left, right, qmap, kmap, *extra)


def signal_level(step):
    return jnp.cos((step / 1000.0 + 0.008) / 1.008 * (math.pi / 2)) ** 2


def ring(size, by):
    return [(i, (i + by) % size) for i in range(size)]


def crossed(value, by, swap):
    perm = []
    for a in range(4):
        for b in range(4):
            for core in range(2):
                if (core == 0) != swap:
                    to = (a, (b + by) % 4)
                else:
                    to = ((a + by) % 4, b)
                perm.append(((a * 4 + b) * 2 + core, (to[0] * 4 + to[1]) * 2 + core))
    return lax.ppermute(value, ("x", "y", "c"), perm)


def on_device(
    kf_query,
    kf_kv,
    cache_kv,
    kf_latent,
    lift_weight,
    gap_latent,
    query_map,
    key_map,
    frame_counts,
    noise_step,
):
    x, y, z, h, c = (lax.axis_index(a) for a in AXES)
    frame = (x * 4 + y) * 4 + z
    up = [(i, i + 1) for i in range(N_FRAME - 1)]
    down = [(j, i) for i, j in up]
    q_prev = lax.ppermute(kf_query, FRAME, up)
    q_next = lax.ppermute(kf_query, FRAME, down)
    line = jnp.stack([lift_weight] + [crossed(lift_weight, d, False) for d in (1, 2, 3)])

    edge = jnp.stack([frame > 0, frame < N_FRAME - 1]).astype(jnp.int32)
    own, stat, latent = own_part(kf_query, kf_kv, cache_kv, kf_latent)
    q_prev, q_next, line, _ = lax.optimization_barrier((q_prev, q_next, line, own))
    to_prev, to_next = far_parts(q_prev, q_next, cache_kv)
    after = lax.ppermute(to_prev, FRAME, down)
    before = lax.ppermute(to_next, FRAME, up)
    pieces = [line] + [crossed(line, e, True) for e in (1, 2, 3)]
    updated, moving = join(edge, latent, own, stat, before, after)

    acts = [moving] + [lax.ppermute(moving, "z", ring(4, d)) for d in (1, 2, 3)]
    info = jnp.stack([x, y, z, c]).astype(jnp.int32)
    keep, send = lift(info, acts, pieces)
    parts = (keep + lax.ppermute(send, "c", ring(2, 1)).astype(F32)).astype(BF)
    parts = lax.all_to_all(parts, ("z", "h"), 0, 0, tiled=False)

    gaps, frames, tokf, width = gap_latent.shape
    lifted, initial = combine(parts, tokf)
    following = lax.ppermute(initial, FRAME, down)

    step = noise_step[0].astype(F32)
    now = signal_level(step)
    then = signal_level(step - STRIDE)
    slots = jnp.arange(frames, dtype=jnp.int32)[None]
    counts = frame_counts[:, None]
    along = (slots + 1).astype(F32) / (counts + 1).astype(F32)
    live = slots < counts
    keep = jnp.where(live, jnp.sqrt(then) / jnp.sqrt(now), 0.0)
    move = jnp.where(
        live, jnp.sqrt(1.0 - then) - jnp.sqrt(then) * jnp.sqrt(1.0 - now) / jnp.sqrt(now), 0.0
    )
    tables = (frame_counts, along, keep, move)
    last = gaps - 1
    out = denoise(0, last, tables, gap_latent, lifted, lifted, 1, query_map, key_map)
    out = denoise(
        last, 1, tables, gap_latent, lifted, following, 0, query_map, key_map, into=out
    )
    return updated, out


def solution(mesh):
    fine = Mesh(mesh.devices.reshape(SIZES), AXES)
    mp = ("h", "c")
    placed = (
        P(FRAME, mp),
        P(None, FRAME, mp),
        P(None, FRAME, mp),
        P(FRAME, mp),
        P(mp, FRAME),
        P(FRAME, None, None, mp),
        P(mp, None, None),
        P(mp, None, None),
        P(FRAME),
        P(),
    )
    return jax.shard_map(
        on_device,
        mesh=fine,
        in_specs=placed,
        out_specs=(P(FRAME, mp), P(FRAME, None, None, mp)),
        check_vma=False,
    )
```

```python
import functools
import math

import jax
import jax.numpy as jnp
from jax import lax
from jax.experimental import pallas as pl
from jax.experimental.pallas import tpu as pltpu
from jax.sharding import Mesh
from jax.sharding import PartitionSpec as P

HD = 128
STRIDE = 200
NEG = -1e30
BF = jnp.bfloat16
F32 = jnp.float32
SCALE = HD ** (-0.5)
SIZES = (4, 4, 4, 2, 2)
AXES = ("x", "y", "z", "h", "c")
FRAME = ("x", "y", "z")
N_FRAME = 64


def nt(a, b):
    return lax.dot_general(a, b, (((1,), (1,)), ((), ())), preferred_element_type=F32)


def tn(a, b):
    return lax.dot_general(a, b, (((0,), (0,)), ((), ())), preferred_element_type=F32)


def nn(a, b):
    return jnp.dot(a, b, preferred_element_type=F32)


def part_of(query, pairs, cols):
    scores = [nt(query, kv[0, :, cols]) for kv in pairs]
    top = functools.reduce(jnp.maximum, [jnp.max(s, axis=1, keepdims=True) for s in scores])
    probs = [jnp.exp((s - top) * SCALE) for s in scores]
    total = sum(jnp.sum(p, axis=1, keepdims=True) for p in probs)
    mixed = sum(nn(p.astype(BF), kv[1, :, cols]) for p, kv in zip(probs, pairs))
    return mixed * (1.0 / total), top * SCALE + jnp.log(total)


def own_kernel(q, kv, own, latent, out, logs, kept):
    step = pl.program_id(0)
    lane = lax.broadcasted_iota(jnp.int32, logs.shape, 1)

    @pl.when(step == 0)
    def _():
        logs[...] = jnp.zeros(logs.shape, F32)

    count = q.shape[1] // HD
    for h in range(count):
        cols = slice(h * HD, (h + 1) * HD)
        mixed, log = part_of(q[:, cols], (own, kv), cols)
        out[:, cols] = mixed
        logs[...] = jnp.where(lane == step * count + h, log, logs[...])
    kept[...] = latent[...]


def own_part(q, kv, own, latent):
    rows, width = q.shape
    ctx = own.shape[1]
    keys = kv.shape[1] + ctx
    step = 2 * HD
    flat = pl.BlockSpec((rows, step), lambda i: (0, i))
    return pl.pallas_call(
        own_kernel,
        grid=(width // step,),
        in_specs=[
            flat,
            pl.BlockSpec((2, rows, step), lambda i: (0, 0, i)),
            pl.BlockSpec((2, ctx, step), lambda i: (0, 0, i)),
            flat,
        ],
        out_specs=(flat, pl.BlockSpec((rows, HD), lambda i: (0, 0)), flat),
        out_shape=(
            jax.ShapeDtypeStruct((rows, width), F32),
            jax.ShapeDtypeStruct((rows, HD), F32),
            jax.ShapeDtypeStruct((rows, width), BF),
        ),
        cost_estimate=pl.CostEstimate(
            flops=4 * rows * width * keys,
            bytes_accessed=4 * keys * width + 6 * rows * width,
            transcendentals=rows * (width // HD) * keys,
        ),
        compiler_params=pltpu.CompilerParams(vmem_limit_bytes=56 << 20),
        name="own_part",
    )(q, kv, own, latent)


def far_kernel(q_a, q_b, own, out_a, out_b):
    rows, width = q_a.shape
    heads = width // HD
    lane = lax.broadcasted_iota(jnp.int32, (2 * rows, HD), 1)
    logs = jnp.zeros((2 * rows, HD), F32)
    for h in range(heads):
        cols = slice(h * HD, (h + 1) * HD)
        query = jnp.concatenate([q_a[:, cols], q_b[:, cols]], axis=0)
        mixed, log = part_of(query, (own,), cols)
        out_a[:, cols] = mixed[:rows].astype(BF)
        out_b[:, cols] = mixed[rows:].astype(BF)
        for k in range(3):
            piece = log.astype(BF).astype(F32)
            logs = jnp.where(lane == k * heads + h, piece, logs)
            log = log - piece
    out_a[:, width:] = logs[:rows].astype(BF)
    out_b[:, width:] = logs[rows:].astype(BF)


def far_parts(q_a, q_b, own):
    rows, width = q_a.shape
    keys = own.shape[1]
    shape = jax.ShapeDtypeStruct((rows, width + HD), BF)
    return pl.pallas_call(
        far_kernel,
        out_shape=(shape, shape),
        cost_estimate=pl.CostEstimate(
            flops=8 * rows * width * keys,
            bytes_accessed=4 * keys * width + 8 * rows * width,
            transcendentals=2 * rows * (width // HD) * keys,
        ),
        compiler_params=pltpu.CompilerParams(vmem_limit_bytes=16 << 20),
        name="far_parts",
    )(q_a, q_b, own)


def join_kernel(edge, latent, own, stat, before, after, out, moving):
    rows, width = latent.shape
    heads = width // HD

    def log_of(part, there):
        logs = part[:, width:].astype(F32)
        logs = logs + pltpu.roll(logs, HD - heads, 1) + pltpu.roll(logs, HD - 2 * heads, 1)
        return jnp.where(there, logs, NEG)

    logs = (stat[...], log_of(before, edge[0] > 0), log_of(after, edge[1] > 0))
    top = functools.reduce(jnp.maximum, logs)
    share = [jnp.exp(v - top) for v in logs]
    inverse = 1.0 / (share[0] + share[1] + share[2])
    share = [v * inverse for v in share]
    for h in range(heads):
        cols = slice(h * HD, (h + 1) * HD)
        one = slice(h, h + 1)
        attn = (
            own[:, cols] * share[0][:, one]
            + before[:, cols].astype(F32) * share[1][:, one]
            + after[:, cols].astype(F32) * share[2][:, one]
        )
        total = (latent[:, cols].astype(F32) + attn).astype(BF)
        out[:, cols] = total
        moving[:, cols] = total


def join(edge, latent, own, stat, before, after):
    rows, width = latent.shape
    vmem = pl.BlockSpec(memory_space=pltpu.VMEM)
    return pl.pallas_call(
        join_kernel,
        in_specs=[pl.BlockSpec(memory_space=pltpu.SMEM)] + [vmem] * 5,
        out_shape=(jax.ShapeDtypeStruct((rows, width), BF),) * 2,
        cost_estimate=pl.CostEstimate(
            flops=8 * rows * width, bytes_accessed=12 * rows * width, transcendentals=4 * rows * HD
        ),
        compiler_params=pltpu.CompilerParams(vmem_limit_bytes=56 << 20),
        name="join",
    )(edge, latent, own, stat, before, after)


def lift_kernel(info, *refs):
    acts, pieces = refs[0:4], refs[4:8]
    keep, send, rows = refs[8:]
    x, y, z, c = info[0], info[1], info[2], info[3]
    frame_rows = acts[0].shape[0]
    for d in range(4):
        rows[d * frame_rows : (d + 1) * frame_rows, :] = acts[d][...]
    for e in range(4):
        for pair in range(2):
            total = nn(
                rows[...],
                jnp.concatenate([pieces[e][2 * pair], pieces[e][2 * pair + 1]], axis=1),
            )
            for k in range(2):
                d = 2 * pair + k
                head_x = lax.rem(x + 4 - jnp.where(c == 0, e, d), 4)
                head_y = lax.rem(y + 4 - jnp.where(c == 0, d, e), 4)
                mine = lax.rem(head_x, 2) == c
                cols = pl.ds(pl.multiple_of(head_y * HD, HD), HD)

                def put(out, cast):
                    for f in range(4):
                        to = lax.rem(z + 4 - f, 4) * 2 + head_x // 2
                        part = total[f * frame_rows : (f + 1) * frame_rows]
                        out[to, :, cols] = cast(part[:, k * HD : (k + 1) * HD])

                @pl.when(mine)
                def _():
                    put(keep, lambda v: v)

                @pl.when(jnp.logical_not(mine))
                def _():
                    put(send, lambda v: v.astype(BF))


def lift(info, acts, pieces):
    rows, width = acts[0].shape
    vmem = pl.BlockSpec(memory_space=pltpu.VMEM)
    return pl.pallas_call(
        lift_kernel,
        in_specs=[pl.BlockSpec(memory_space=pltpu.SMEM)] + [vmem] * 8,
        out_shape=(
            jax.ShapeDtypeStruct((8, rows, 4 * HD), F32),
            jax.ShapeDtypeStruct((8, rows, 4 * HD), BF),
        ),
        scratch_shapes=[pltpu.VMEM((4 * rows, width), BF)],
        compiler_params=pltpu.CompilerParams(vmem_limit_bytes=24 << 20),
        cost_estimate=pl.CostEstimate(
            flops=2 * 4 * rows * width * 16 * HD,
            bytes_accessed=2 * (16 * width * HD + 4 * rows * width + 48 * rows * HD),
            transcendentals=0,
        ),
        name="lift",
    )(info, *acts, *pieces)


def combine_kernel(parts, out, first):
    for y in range(4):
        cols = slice(y * HD, (y + 1) * HD)
        for z in range(4):
            place = slice((y * 4 + z) * HD, (y * 4 + z + 1) * HD)
            total = parts[2 * z, :, cols].astype(F32) + parts[2 * z + 1, :, cols].astype(F32)
            total = total.astype(BF)
            out[:, place] = total
            first[:, place] = total[: first.shape[0]]


def combine(parts, tokf):
    rows = parts.shape[1]
    width = 4 * parts.shape[2]
    return pl.pallas_call(
        combine_kernel,
        out_shape=(
            jax.ShapeDtypeStruct((rows, width), BF),
            jax.ShapeDtypeStruct((tokf, width), BF),
        ),
        cost_estimate=pl.CostEstimate(
            flops=2 * rows * width, bytes_accessed=6 * rows * width, transcendentals=0
        ),
        compiler_params=pltpu.CompilerParams(vmem_limit_bytes=16 << 20),
        name="combine",
    )(parts)


def gap_kernel(first, count, along, keep, move, latent, left, right, qmap, kmap, *rest):
    out = rest[-1]
    gap = first + pl.program_id(0)
    heads = qmap.shape[0]
    frames, tokf = latent.shape[1], latent.shape[2]
    toks = frames * tokf
    live = count[gap] * tokf
    bias = jnp.where(lax.broadcasted_iota(jnp.int32, (toks, 1), 0) < live, 0.0, NEG).astype(F32)

    def map_rows(h):
        cols = slice(h * HD, (h + 1) * HD)
        lo, hi = left[:, cols], right[:, cols]
        lo32, hi32 = lo.astype(F32), hi.astype(F32)
        tokens = [
            (
                latent[0, j, :, cols].astype(F32)
                + (1.0 - along[gap, j]) * lo32
                + along[gap, j] * hi32
            ).astype(BF)
            for j in range(frames)
        ]
        values = jnp.concatenate(tokens + [lo, hi], axis=0)
        mapped = nn(values, jnp.concatenate([qmap[h], kmap[h]], axis=1)).astype(BF)
        return values, mapped[:toks, :HD], mapped[:, HD:]

    def score(values, query, key):
        scores = nt(key, query)
        return values, jnp.concatenate([scores[:toks] + bias, scores[toks:]], axis=0)

    def finish(h, values, scores):
        cols = slice(h * HD, (h + 1) * HD)
        top = jnp.max(scores, axis=0, keepdims=True)
        probs = jnp.exp2((scores - top) * (SCALE * math.log2(math.e)))
        total = jnp.sum(probs, axis=0, keepdims=True)
        mixed = tn(values, probs.astype(BF))
        guess = jnp.transpose(mixed * (1.0 / total))
        for j in range(frames):
            rows = slice(j * tokf, (j + 1) * tokf)
            out[0, j, :, cols] = (
                latent[0, j, :, cols].astype(F32) * keep[gap, j] + guess[rows] * move[gap, j]
            ).astype(BF)

    mapped, scored = {}, {}
    for t in range(heads + 2):
        if t < heads:
            mapped[t] = map_rows(t)
        if 0 <= t - 1 < heads:
            scored[t - 1] = score(*mapped.pop(t - 1))
        if 0 <= t - 2 < heads:
            finish(t - 2, *scored.pop(t - 2))


def denoise(first, gaps, tables, latent, left, right, right_at, qmap, kmap, into=None):
    _, frames, tokf, width = latent.shape
    heads = width // HD
    spot = pl.BlockSpec((1, frames, tokf, width), lambda g, *s: (first + g, 0, 0, 0))
    before = pl.BlockSpec((tokf, width), lambda g, *s: (first + g, 0))
    after = pl.BlockSpec((tokf, width), lambda g, *s: (right_at + g, 0))
    maps = pl.BlockSpec((heads, HD, HD), lambda g, *s: (0, 0, 0))
    extra = [] if into is None else [into]
    specs = [spot, before, after, maps, maps] + [pl.BlockSpec(memory_space=pl.ANY)] * len(extra)
    toks = frames * tokf
    return pl.pallas_call(
        functools.partial(gap_kernel, first),
        grid_spec=pltpu.PrefetchScalarGridSpec(
            num_scalar_prefetch=4, grid=(gaps,), in_specs=specs, out_specs=spot
        ),
        out_shape=jax.ShapeDtypeStruct(latent.shape, BF),
        input_output_aliases={9: 0} if extra else {},
        compiler_params=pltpu.CompilerParams(vmem_limit_bytes=52 << 20),
        cost_estimate=pl.CostEstimate(
            flops=gaps * 2 * toks * width * (2 * HD + 2 * (toks + 2 * tokf)),
            bytes_accessed=4 * gaps * toks * width,
            transcendentals=gaps * heads * toks * (toks + 2 * tokf),
        ),
        name=f"denoise_{first}",
    )(*tables, latent, left, right, qmap, kmap, *extra)


def signal_level(step):
    return jnp.cos((step / 1000.0 + 0.008) / 1.008 * (math.pi / 2)) ** 2


def ring(size, by):
    return [(i, (i + by) % size) for i in range(size)]


def crossed(value, by, swap):
    perm = []
    for a in range(4):
        for b in range(4):
            for core in range(2):
                if (core == 0) != swap:
                    to = (a, (b + by) % 4)
                else:
                    to = ((a + by) % 4, b)
                perm.append(((a * 4 + b) * 2 + core, (to[0] * 4 + to[1]) * 2 + core))
    return lax.ppermute(value, ("x", "y", "c"), perm)


def on_device(
    kf_query,
    kf_kv,
    cache_kv,
    kf_latent,
    lift_weight,
    gap_latent,
    query_map,
    key_map,
    frame_counts,
    noise_step,
):
    x, y, z, h, c = (lax.axis_index(a) for a in AXES)
    frame = (x * 4 + y) * 4 + z
    up = [(i, i + 1) for i in range(N_FRAME - 1)]
    down = [(j, i) for i, j in up]
    q_prev = lax.ppermute(kf_query, FRAME, up)
    q_next = lax.ppermute(kf_query, FRAME, down)
    line = jnp.stack([lift_weight] + [crossed(lift_weight, d, False) for d in (1, 2, 3)])

    edge = jnp.stack([frame > 0, frame < N_FRAME - 1]).astype(jnp.int32)
    q_prev, q_next, line = lax.optimization_barrier((q_prev, q_next, line))
    to_prev, to_next = far_parts(q_prev, q_next, cache_kv)
    query, _ = lax.optimization_barrier((kf_query, to_prev))
    own, stat, latent = own_part(query, kf_kv, cache_kv, kf_latent)
    after = lax.ppermute(to_prev, FRAME, down)
    before = lax.ppermute(to_next, FRAME, up)
    pieces = [line] + [crossed(line, e, True) for e in (1, 2, 3)]
    updated, moving = join(edge, latent, own, stat, before, after)

    moving, pieces[1] = lax.optimization_barrier((moving, pieces[1]))
    acts = [moving] + [lax.ppermute(moving, "z", ring(4, d)) for d in (1, 2, 3)]
    info = jnp.stack([x, y, z, c]).astype(jnp.int32)
    keep, send = lift(info, acts, pieces)
    parts = (keep + lax.ppermute(send, "c", ring(2, 1)).astype(F32)).astype(BF)
    parts = lax.all_to_all(parts, ("z", "h"), 0, 0, tiled=False)

    gaps, frames, tokf, width = gap_latent.shape
    lifted, initial = combine(parts, tokf)
    following = lax.ppermute(initial, FRAME, down)

    step = noise_step[0].astype(F32)
    now = signal_level(step)
    then = signal_level(step - STRIDE)
    slots = jnp.arange(frames, dtype=jnp.int32)[None]
    counts = frame_counts[:, None]
    along = (slots + 1).astype(F32) / (counts + 1).astype(F32)
    live = slots < counts
    keep = jnp.where(live, jnp.sqrt(then) / jnp.sqrt(now), 0.0)
    move = jnp.where(
        live, jnp.sqrt(1.0 - then) - jnp.sqrt(then) * jnp.sqrt(1.0 - now) / jnp.sqrt(now), 0.0
    )
    tables = (frame_counts, along, keep, move)
    last = gaps - 1
    out = denoise(0, last, tables, gap_latent, lifted, lifted, 1, query_map, key_map)
    out = denoise(
        last, 1, tables, gap_latent, lifted, following, 0, query_map, key_map, into=out
    )
    return updated, out


def solution(mesh):
    fine = Mesh(mesh.devices.reshape(SIZES), AXES)
    mp = ("h", "c")
    placed = (
        P(FRAME, mp),
        P(None, FRAME, mp),
        P(None, FRAME, mp),
        P(FRAME, mp),
        P(mp, FRAME),
        P(FRAME, None, None, mp),
        P(mp, None, None),
        P(mp, None, None),
        P(FRAME),
        P(),
    )
    return jax.shard_map(
        on_device,
        mesh=fine,
        in_specs=placed,
        out_specs=(P(FRAME, mp), P(FRAME, None, None, mp)),
        check_vma=False,
    )
```

```python
import functools
import math

import jax
import jax.numpy as jnp
from jax import lax
from jax.experimental import pallas as pl
from jax.experimental.pallas import tpu as pltpu
from jax.sharding import Mesh
from jax.sharding import PartitionSpec as P

HD = 128
STRIDE = 200
NEG = -1e30
BF = jnp.bfloat16
F32 = jnp.float32
SCALE = HD ** (-0.5)
SIZES = (4, 4, 4, 2, 2)
AXES = ("x", "y", "z", "h", "c")
FRAME = ("x", "y", "z")
N_FRAME = 64


def nt(a, b):
    return lax.dot_general(a, b, (((1,), (1,)), ((), ())), preferred_element_type=F32)


def tn(a, b):
    return lax.dot_general(a, b, (((0,), (0,)), ((), ())), preferred_element_type=F32)


def nn(a, b):
    return jnp.dot(a, b, preferred_element_type=F32)


def part_of(query, pairs, cols):
    scores = [nt(query, kv[0, :, cols]) for kv in pairs]
    top = functools.reduce(jnp.maximum, [jnp.max(s, axis=1, keepdims=True) for s in scores])
    probs = [jnp.exp((s - top) * SCALE) for s in scores]
    total = sum(jnp.sum(p, axis=1, keepdims=True) for p in probs)
    mixed = sum(nn(p.astype(BF), kv[1, :, cols]) for p, kv in zip(probs, pairs))
    return mixed * (1.0 / total), top * SCALE + jnp.log(total)


def own_kernel(q, kv, own, latent, out, logs, kept):
    step = pl.program_id(0)
    lane = lax.broadcasted_iota(jnp.int32, logs.shape, 1)

    @pl.when(step == 0)
    def _():
        logs[...] = jnp.zeros(logs.shape, F32)

    count = q.shape[1] // HD
    for h in range(count):
        cols = slice(h * HD, (h + 1) * HD)
        mixed, log = part_of(q[:, cols], (own, kv), cols)
        out[:, cols] = mixed
        logs[...] = jnp.where(lane == step * count + h, log, logs[...])
    kept[...] = latent[...]


def own_part(q, kv, own, latent):
    rows, width = q.shape
    ctx = own.shape[1]
    keys = kv.shape[1] + ctx
    step = 2 * HD
    flat = pl.BlockSpec((rows, step), lambda i: (0, i))
    return pl.pallas_call(
        own_kernel,
        grid=(width // step,),
        in_specs=[
            flat,
            pl.BlockSpec((2, rows, step), lambda i: (0, 0, i)),
            pl.BlockSpec((2, ctx, step), lambda i: (0, 0, i)),
            flat,
        ],
        out_specs=(flat, pl.BlockSpec((rows, HD), lambda i: (0, 0)), flat),
        out_shape=(
            jax.ShapeDtypeStruct((rows, width), F32),
            jax.ShapeDtypeStruct((rows, HD), F32),
            jax.ShapeDtypeStruct((rows, width), BF),
        ),
        cost_estimate=pl.CostEstimate(
            flops=4 * rows * width * keys,
            bytes_accessed=4 * keys * width + 6 * rows * width,
            transcendentals=rows * (width // HD) * keys,
        ),
        compiler_params=pltpu.CompilerParams(vmem_limit_bytes=56 << 20),
        name="own_part",
    )(q, kv, own, latent)


def far_kernel(q_a, q_b, own, out_a, out_b):
    rows, width = q_a.shape
    heads = width // HD
    lane = lax.broadcasted_iota(jnp.int32, (2 * rows, HD), 1)
    logs = jnp.zeros((2 * rows, HD), F32)
    for h in range(heads):
        cols = slice(h * HD, (h + 1) * HD)
        query = jnp.concatenate([q_a[:, cols], q_b[:, cols]], axis=0)
        mixed, log = part_of(query, (own,), cols)
        out_a[:, cols] = mixed[:rows].astype(BF)
        out_b[:, cols] = mixed[rows:].astype(BF)
        for k in range(3):
            piece = log.astype(BF).astype(F32)
            logs = jnp.where(lane == k * heads + h, piece, logs)
            log = log - piece
    out_a[:, width:] = logs[:rows].astype(BF)
    out_b[:, width:] = logs[rows:].astype(BF)


def far_parts(q_a, q_b, own):
    rows, width = q_a.shape
    keys = own.shape[1]
    shape = jax.ShapeDtypeStruct((rows, width + HD), BF)
    return pl.pallas_call(
        far_kernel,
        out_shape=(shape, shape),
        cost_estimate=pl.CostEstimate(
            flops=8 * rows * width * keys,
            bytes_accessed=4 * keys * width + 8 * rows * width,
            transcendentals=2 * rows * (width // HD) * keys,
        ),
        compiler_params=pltpu.CompilerParams(vmem_limit_bytes=16 << 20),
        name="far_parts",
    )(q_a, q_b, own)


def join_kernel(edge, latent, own, stat, before, after, out, moving):
    rows, width = latent.shape
    heads = width // HD

    def log_of(part, there):
        logs = part[:, width:].astype(F32)
        logs = logs + pltpu.roll(logs, HD - heads, 1) + pltpu.roll(logs, HD - 2 * heads, 1)
        return jnp.where(there, logs, NEG)

    logs = (stat[...], log_of(before, edge[0] > 0), log_of(after, edge[1] > 0))
    top = functools.reduce(jnp.maximum, logs)
    share = [jnp.exp(v - top) for v in logs]
    inverse = 1.0 / (share[0] + share[1] + share[2])
    share = [v * inverse for v in share]
    for h in range(heads):
        cols = slice(h * HD, (h + 1) * HD)
        one = slice(h, h + 1)
        attn = (
            own[:, cols] * share[0][:, one]
            + before[:, cols].astype(F32) * share[1][:, one]
            + after[:, cols].astype(F32) * share[2][:, one]
        )
        total = (latent[:, cols].astype(F32) + attn).astype(BF)
        out[:, cols] = total
        moving[:, cols] = total


def join(edge, latent, own, stat, before, after):
    rows, width = latent.shape
    vmem = pl.BlockSpec(memory_space=pltpu.VMEM)
    return pl.pallas_call(
        join_kernel,
        in_specs=[pl.BlockSpec(memory_space=pltpu.SMEM)] + [vmem] * 5,
        out_shape=(jax.ShapeDtypeStruct((rows, width), BF),) * 2,
        cost_estimate=pl.CostEstimate(
            flops=8 * rows * width, bytes_accessed=12 * rows * width, transcendentals=4 * rows * HD
        ),
        compiler_params=pltpu.CompilerParams(vmem_limit_bytes=56 << 20),
        name="join",
    )(edge, latent, own, stat, before, after)


def lift_kernel(info, *refs):
    acts, pieces = refs[0:4], refs[4:8]
    keep, send, rows = refs[8:]
    x, y, z, c = info[0], info[1], info[2], info[3]
    frame_rows = acts[0].shape[0]
    for d in range(4):
        rows[d * frame_rows : (d + 1) * frame_rows, :] = acts[d][...]
    for e in range(4):
        for pair in range(2):
            total = nn(
                rows[...],
                jnp.concatenate([pieces[e][2 * pair], pieces[e][2 * pair + 1]], axis=1),
            )
            for k in range(2):
                d = 2 * pair + k
                head_x = lax.rem(x + 4 - jnp.where(c == 0, e, d), 4)
                head_y = lax.rem(y + 4 - jnp.where(c == 0, d, e), 4)
                mine = lax.rem(head_x, 2) == c
                cols = pl.ds(pl.multiple_of(head_y * HD, HD), HD)

                def put(out, cast):
                    for f in range(4):
                        to = lax.rem(z + 4 - f, 4) * 2 + head_x // 2
                        part = total[f * frame_rows : (f + 1) * frame_rows]
                        out[to, :, cols] = cast(part[:, k * HD : (k + 1) * HD])

                @pl.when(mine)
                def _():
                    put(keep, lambda v: v)

                @pl.when(jnp.logical_not(mine))
                def _():
                    put(send, lambda v: v.astype(BF))


def lift(info, acts, pieces):
    rows, width = acts[0].shape
    vmem = pl.BlockSpec(memory_space=pltpu.VMEM)
    return pl.pallas_call(
        lift_kernel,
        in_specs=[pl.BlockSpec(memory_space=pltpu.SMEM)] + [vmem] * 8,
        out_shape=(
            jax.ShapeDtypeStruct((8, rows, 4 * HD), F32),
            jax.ShapeDtypeStruct((8, rows, 4 * HD), BF),
        ),
        scratch_shapes=[pltpu.VMEM((4 * rows, width), BF)],
        compiler_params=pltpu.CompilerParams(vmem_limit_bytes=56 << 20),
        cost_estimate=pl.CostEstimate(
            flops=2 * 4 * rows * width * 16 * HD,
            bytes_accessed=2 * (16 * width * HD + 4 * rows * width + 48 * rows * HD),
            transcendentals=0,
        ),
        name="lift",
    )(info, *acts, *pieces)


def combine_kernel(parts, out, first):
    for y in range(4):
        cols = slice(y * HD, (y + 1) * HD)
        for z in range(4):
            place = slice((y * 4 + z) * HD, (y * 4 + z + 1) * HD)
            total = parts[2 * z, :, cols].astype(F32) + parts[2 * z + 1, :, cols].astype(F32)
            total = total.astype(BF)
            out[:, place] = total
            first[:, place] = total[: first.shape[0]]


def combine(parts, tokf):
    rows = parts.shape[1]
    width = 4 * parts.shape[2]
    return pl.pallas_call(
        combine_kernel,
        out_shape=(
            jax.ShapeDtypeStruct((rows, width), BF),
            jax.ShapeDtypeStruct((tokf, width), BF),
        ),
        cost_estimate=pl.CostEstimate(
            flops=2 * rows * width, bytes_accessed=6 * rows * width, transcendentals=0
        ),
        compiler_params=pltpu.CompilerParams(vmem_limit_bytes=16 << 20),
        name="combine",
    )(parts)


def gap_kernel(first, count, along, keep, move, latent, left, right, qmap, kmap, *rest):
    out = rest[-1]
    gap = first + pl.program_id(0)
    heads = qmap.shape[0]
    frames, tokf = latent.shape[1], latent.shape[2]
    toks = frames * tokf
    live = count[gap] * tokf
    bias = jnp.where(lax.broadcasted_iota(jnp.int32, (toks, 1), 0) < live, 0.0, NEG).astype(F32)

    def map_rows(h):
        cols = slice(h * HD, (h + 1) * HD)
        lo, hi = left[:, cols], right[:, cols]
        lo32, hi32 = lo.astype(F32), hi.astype(F32)
        tokens = [
            (
                latent[0, j, :, cols].astype(F32)
                + (1.0 - along[gap, j]) * lo32
                + along[gap, j] * hi32
            ).astype(BF)
            for j in range(frames)
        ]
        values = jnp.concatenate(tokens + [lo, hi], axis=0)
        mapped = nn(values, jnp.concatenate([qmap[h], kmap[h]], axis=1)).astype(BF)
        return values, mapped[:toks, :HD], mapped[:, HD:]

    def score(values, query, key):
        scores = nt(key, query)
        return values, jnp.concatenate([scores[:toks] + bias, scores[toks:]], axis=0)

    def finish(h, values, scores):
        cols = slice(h * HD, (h + 1) * HD)
        top = jnp.max(scores, axis=0, keepdims=True)
        probs = jnp.exp2((scores - top) * (SCALE * math.log2(math.e)))
        total = jnp.sum(probs, axis=0, keepdims=True)
        mixed = tn(values, probs.astype(BF))
        guess = jnp.transpose(mixed * (1.0 / total))
        for j in range(frames):
            rows = slice(j * tokf, (j + 1) * tokf)
            out[0, j, :, cols] = (
                latent[0, j, :, cols].astype(F32) * keep[gap, j] + guess[rows] * move[gap, j]
            ).astype(BF)

    mapped, scored = {}, {}
    for t in range(heads + 2):
        if t < heads:
            mapped[t] = map_rows(t)
        if 0 <= t - 1 < heads:
            scored[t - 1] = score(*mapped.pop(t - 1))
        if 0 <= t - 2 < heads:
            finish(t - 2, *scored.pop(t - 2))


def denoise(first, gaps, tables, latent, left, right, right_at, qmap, kmap, into=None):
    _, frames, tokf, width = latent.shape
    heads = width // HD
    spot = pl.BlockSpec((1, frames, tokf, width), lambda g, *s: (first + g, 0, 0, 0))
    before = pl.BlockSpec((tokf, width), lambda g, *s: (first + g, 0))
    after = pl.BlockSpec((tokf, width), lambda g, *s: (right_at + g, 0))
    maps = pl.BlockSpec((heads, HD, HD), lambda g, *s: (0, 0, 0))
    extra = [] if into is None else [into]
    specs = [spot, before, after, maps, maps] + [pl.BlockSpec(memory_space=pl.ANY)] * len(extra)
    toks = frames * tokf
    return pl.pallas_call(
        functools.partial(gap_kernel, first),
        grid_spec=pltpu.PrefetchScalarGridSpec(
            num_scalar_prefetch=4, grid=(gaps,), in_specs=specs, out_specs=spot
        ),
        out_shape=jax.ShapeDtypeStruct(latent.shape, BF),
        input_output_aliases={9: 0} if extra else {},
        compiler_params=pltpu.CompilerParams(vmem_limit_bytes=52 << 20),
        cost_estimate=pl.CostEstimate(
            flops=gaps * 2 * toks * width * (2 * HD + 2 * (toks + 2 * tokf)),
            bytes_accessed=4 * gaps * toks * width,
            transcendentals=gaps * heads * toks * (toks + 2 * tokf),
        ),
        name=f"denoise_{first}",
    )(*tables, latent, left, right, qmap, kmap, *extra)


def signal_level(step):
    return jnp.cos((step / 1000.0 + 0.008) / 1.008 * (math.pi / 2)) ** 2


def ring(size, by):
    return [(i, (i + by) % size) for i in range(size)]


def crossed(value, by, swap):
    perm = []
    for a in range(4):
        for b in range(4):
            for core in range(2):
                if (core == 0) != swap:
                    to = (a, (b + by) % 4)
                else:
                    to = ((a + by) % 4, b)
                perm.append(((a * 4 + b) * 2 + core, (to[0] * 4 + to[1]) * 2 + core))
    return lax.ppermute(value, ("x", "y", "c"), perm)


def on_device(
    kf_query,
    kf_kv,
    cache_kv,
    kf_latent,
    lift_weight,
    gap_latent,
    query_map,
    key_map,
    frame_counts,
    noise_step,
):
    x, y, z, h, c = (lax.axis_index(a) for a in AXES)
    frame = (x * 4 + y) * 4 + z
    up = [(i, i + 1) for i in range(N_FRAME - 1)]
    down = [(j, i) for i, j in up]
    q_prev = lax.ppermute(kf_query, FRAME, up)
    q_next = lax.ppermute(kf_query, FRAME, down)
    line = jnp.stack([lift_weight] + [crossed(lift_weight, d, False) for d in (1, 2, 3)])

    edge = jnp.stack([frame > 0, frame < N_FRAME - 1]).astype(jnp.int32)
    q_prev, q_next, line = lax.optimization_barrier((q_prev, q_next, line))
    to_prev, to_next = far_parts(q_prev, q_next, cache_kv)
    query, _ = lax.optimization_barrier((kf_query, to_prev))
    own, stat, latent = own_part(query, kf_kv, cache_kv, kf_latent)
    after = lax.ppermute(to_prev, FRAME, down)
    before = lax.ppermute(to_next, FRAME, up)
    pieces = [line] + [crossed(line, e, True) for e in (1, 2, 3)]
    updated, moving = join(edge, latent, own, stat, before, after)

    moving, pieces[1] = lax.optimization_barrier((moving, pieces[1]))
    acts = [moving] + [lax.ppermute(moving, "z", ring(4, d)) for d in (1, 2, 3)]
    info = jnp.stack([x, y, z, c]).astype(jnp.int32)
    keep, send = lift(info, acts, pieces)
    parts = (keep + lax.ppermute(send, "c", ring(2, 1)).astype(F32)).astype(BF)
    parts = lax.all_to_all(parts, ("z", "h"), 0, 0, tiled=False)

    gaps, frames, tokf, width = gap_latent.shape
    lifted, initial = combine(parts, tokf)
    following = lax.ppermute(initial, FRAME, down)

    step = noise_step[0].astype(F32)
    now = signal_level(step)
    then = signal_level(step - STRIDE)
    slots = jnp.arange(frames, dtype=jnp.int32)[None]
    counts = frame_counts[:, None]
    along = (slots + 1).astype(F32) / (counts + 1).astype(F32)
    live = slots < counts
    keep = jnp.where(live, jnp.sqrt(then) / jnp.sqrt(now), 0.0)
    move = jnp.where(
        live, jnp.sqrt(1.0 - then) - jnp.sqrt(then) * jnp.sqrt(1.0 - now) / jnp.sqrt(now), 0.0
    )
    tables = (frame_counts, along, keep, move)
    last = gaps - 1
    out = denoise(0, last, tables, gap_latent, lifted, lifted, 1, query_map, key_map)
    out = denoise(
        last, 1, tables, gap_latent, lifted, following, 0, query_map, key_map, into=out
    )
    return updated, out


def solution(mesh):
    fine = Mesh(mesh.devices.reshape(SIZES), AXES)
    mp = ("h", "c")
    placed = (
        P(FRAME, mp),
        P(None, FRAME, mp),
        P(None, FRAME, mp),
        P(FRAME, mp),
        P(mp, FRAME),
        P(FRAME, None, None, mp),
        P(mp, None, None),
        P(mp, None, None),
        P(FRAME),
        P(),
    )
    return jax.shard_map(
        on_device,
        mesh=fine,
        in_specs=placed,
        out_specs=(P(FRAME, mp), P(FRAME, None, None, mp)),
        check_vma=False,
    )
```
